32 devices in a mesh: ctx: 16 (over z, y, x), tp: 2 (over core).
Axes of the slice: x: 2, y: 2, z: 4, core: 2. Of those that a mesh axis runs over, the one named last changes fastest.
Arguments:
- q_one: bfloat16 [4096, 8192], P('ctx', 'tp'), may hold values from -6 to 6
- k_one: bfloat16 [4096, 8192], P('ctx', 'tp'), may hold values from -40 to 40, as said below
- v_one: bfloat16 [4096, 8192], P('ctx', 'tp'), may hold values from -6 to 6
- mr_filter: bfloat16 [512, 128], P('tp'), may hold values from -3.535534 to 3.535534
- norm_gain: float32 [8192], P('tp'), may hold values from 0.1 to 1.9
- q_two: bfloat16 [4096, 8192], P('ctx', 'tp'), may hold values from -6 to 6
- k_two: bfloat16 [4096, 8192], P('ctx', 'tp'), may hold values from -6 to 6
- li_rates: float32 [16, 8192], P(None, 'tp'), may hold values from 6.1035156e-05 to 0.03
- li_residues: float32 [16, 8192], P(None, 'tp'), may hold values from -4 to 4
Outputs:
- mixed: bfloat16 [4096, 8192], P('ctx', 'tp')
The draws below stay inside these ranges and needn't reach their ends.
Inputs may be any that keep to these rules, and one draw needn't show every extreme that they name: Each row of k_one has a scale of its own.
All inputs are finite; a program needn't handle non-finite values.
Results may differ from the reference program's by a relative error of at most 0.0057.
Values may be sent and summed in bfloat16 or wider, within the bound.
A program may use at most 128 MiB of HBM per device.

```python
import math
import jax
import jax.numpy as jnp
from jax import lax

D = 8192
TOK_DEV = 256
KMR = 128
MODES = 16
MR_GROUP = 16
SEQ = 4096
MR_FILTERS = 512


def draw_k_one(key, part):
    base_key = jax.random.fold_in(key, 11)
    scale_key = jax.random.fold_in(key, 12)
    base = jnp.clip(jax.random.normal(base_key, (SEQ, D), jnp.float32), -4.0, 4.0)
    row_scale = 10.0 ** jax.random.uniform(scale_key, (SEQ, 1), jnp.float32, 0.0, 1.0)
    return (base * row_scale).astype(jnp.bfloat16)


def draw_mr_filter(key, part):
    base_key = jax.random.fold_in(key, 21)
    base = jnp.clip(jax.random.normal(base_key, (MR_FILTERS, KMR), jnp.float32), -4.0, 4.0)
    ramp = jnp.arange(MR_FILTERS).astype(jnp.float32) / MR_FILTERS
    scaled = base * (10.0 ** ramp)[:, None] / KMR ** 0.5
    return scaled.astype(jnp.bfloat16)


def level_of(key, extent, cuts, smallest, top_value):
    level = 1.0
    for dim, blocks in cuts:
        steps = jax.random.uniform(jax.random.fold_in(jax.random.fold_in(key, 6), dim), (blocks,), jnp.float32, smallest / len(cuts), top_value / len(cuts))
        level = level * jnp.repeat(jnp.exp(steps), extent[dim] // blocks).reshape((-1,) + (1,) * (len(extent) - 1 - dim))
    return level


def scatter_about(own_key, dims, deviation, most, shards=(), kind=jnp.bfloat16):
    values = jax.random.normal(own_key, dims, jnp.float32) * deviation
    if len(shards) > 0:
        values = level_of(own_key, dims, shards, -0.22, 0.18) * values
    return jnp.clip(values, min=-most, max=most).astype(kind)


def setup_inputs(seed: int = 0) -> dict:
    seeds = jax.random.split(jax.random.key(seed), 10)
    return {
        "q_one": scatter_about(seeds[0], (SEQ, D), 1.0, 6.0, ((0, 16), (1, 2))),
        "k_one": draw_k_one(jax.random.fold_in(seeds[9], 71), 0),
        "v_one": scatter_about(seeds[2], (SEQ, D), 1.0, 6.0, ((0, 16), (1, 2))),
        "mr_filter": draw_mr_filter(jax.random.fold_in(seeds[9], 71), 0),
        "norm_gain": jnp.clip(1.0 + 0.18 * jax.random.normal(seeds[4], (D,), jnp.float32), 0.1, 1.9),
        "q_two": scatter_about(seeds[5], (SEQ, D), 1.0, 6.0, ((0, 16), (1, 2))),
        "k_two": scatter_about(seeds[6], (SEQ, D), 1.0, 6.0, ((0, 16), (1, 2))),
        "li_rates": jnp.clip(jnp.exp(math.log(0.03) - 6.1975026 * jax.random.uniform(seeds[7], (MODES, D), jnp.float32) ** level_of(seeds[7], (MODES, D), ((1, 2),), -0.2, 0.2)), 6.103515625e-05, 0.03),
        "li_residues": scatter_about(seeds[8], (MODES, D), 0.25, 4.0, ((1, 2),), jnp.float32),
    }


def join_states(earlier, later):
    return (earlier[0] * later[0], later[0] * earlier[1] + later[1])

def modal_parts(rates, residues, sub_len):
    norm_scale = jnp.sqrt(-jnp.expm1(-2.0 * rates))
    weights = residues * norm_scale
    lags = jnp.arange(sub_len).astype(jnp.float32)
    powers = jnp.exp(-rates[:, None, :] * lags[None, :, None])
    kernel = lax.optimization_barrier(jnp.sum(weights[:, None, :] * powers, axis=0))
    lag_table = jnp.arange(sub_len)[:, None] - jnp.arange(sub_len)[None, :]
    toeplitz = jnp.where((lag_table >= 0)[:, :, None], kernel[jnp.clip(lag_table, 0, sub_len - 1)], 0.0)
    closing_w = powers[:, ::-1, :]
    entry_w = weights[:, None, :] * powers * jnp.exp(-rates)[:, None, :]
    stride_decay = jnp.exp(-rates * sub_len)
    return (toeplitz, closing_w, entry_w, stride_decay)

def local_pass(signal, parts):
    toeplitz, closing_w, entry_w, stride_decay = parts
    inner = jnp.einsum('ijc,bjc->bic', toeplitz, signal, precision=lax.Precision.HIGHEST)
    closing = jnp.einsum('mjc,bjc->bmc', closing_w, signal, precision=lax.Precision.HIGHEST)
    decays = jnp.broadcast_to(stride_decay, closing.shape)
    _, states = lax.associative_scan(join_states, (decays, closing), axis=0)
    return (inner, states)

def finish(inner, states, incoming, rates, parts):
    entry_w = parts[2]
    sub_len = inner.shape[1]
    prior = jnp.concatenate([jnp.zeros_like(states[:1]), states[:-1]], axis=0)
    count = jnp.arange(inner.shape[0]).astype(jnp.float32)[:, None, None]
    prior = prior + jnp.exp(-rates[None] * (sub_len * count)) * incoming[None]
    return inner + jnp.einsum('mic,bmc->bic', entry_w, prior, precision=lax.Precision.HIGHEST)

def reference(q_one, k_one, v_one, mr_filter, norm_gain, q_two, k_two, li_rates, li_residues):
    u_one = (k_one.astype(jnp.float32) * v_one.astype(jnp.float32)).astype(jnp.bfloat16)
    taps = mr_filter.shape[1]
    chan_taps = jnp.repeat(mr_filter.astype(jnp.float32), MR_GROUP, axis=0).T
    padded = jnp.concatenate([jnp.zeros((taps - 1, D), jnp.float32), u_one.astype(jnp.float32)], axis=0)

    def add_tap(index, total):
        piece = lax.dynamic_slice_in_dim(padded, taps - 1 - index, SEQ, 0)
        return total + piece * lax.dynamic_index_in_dim(chan_taps, index, 0, keepdims=False)[None, :]
    conv_one = lax.fori_loop(0, taps, add_tap, jnp.zeros((SEQ, D), jnp.float32))
    z_one = q_one.astype(jnp.float32) * conv_one
    squares = lax.optimization_barrier(jnp.sum(z_one * z_one, axis=1))
    scaled = z_one * lax.rsqrt(squares / D + 1e-06)[:, None] * norm_gain[None, :]
    u_two = (k_two.astype(jnp.float32) * scaled).astype(jnp.bfloat16)
    sub_len = min(32, TOK_DEV)
    parts = modal_parts(li_rates, li_residues, sub_len)
    signal = u_two.astype(jnp.float32).reshape(SEQ // sub_len, sub_len, D)
    inner, states = local_pass(signal, parts)
    conv_two = finish(inner, states, jnp.zeros((MODES, D), jnp.float32), li_rates, parts).reshape(SEQ, D)
    return (q_two.astype(jnp.float32) * conv_two).astype(jnp.bfloat16)
```

```python
import functools
import jax
import jax.numpy as jnp
from jax import lax
from jax.experimental import pallas as pl
from jax.experimental.pallas import tpu as pltpu
from jax.sharding import PartitionSpec as P

D = 8192
LANES = 128
SEGS = 8
F32 = jnp.float32
BF16 = jnp.bfloat16


def toeplitz_rows(tap_rows, groups, store):
    taps = tap_rows.shape[1]
    row = lax.broadcasted_iota(jnp.int32, (taps, taps), 0)
    col = lax.broadcasted_iota(jnp.int32, (taps, taps), 1)
    later = col > row
    for g in range(groups):
        base = jnp.broadcast_to(tap_rows[g : g + 1, :], (8, taps))
        base = pltpu.roll(base, 0, 1, stride=1, stride_axis=0)
        tiles = [base if i == 0 else pltpu.roll(base, 8 * i, 1) for i in range(taps // 8)]
        circulant = jnp.concatenate(tiles, axis=0)
        store[g * taps : (g + 1) * taps, :taps] = jnp.where(later, circulant, 0.0).astype(BF16)
        store[g * taps : (g + 1) * taps, taps:] = jnp.where(later, 0.0, circulant).astype(BF16)


def conv_kernel(q_ref, k_ref, v_ref, halo_ref, tap_ref, z_ref, sq_ref, table):
    taps = tap_ref.shape[1]
    length = q_ref.shape[0]
    blocks = length // taps
    groups = tap_ref.shape[0]
    width = LANES // groups
    toeplitz_rows(tap_ref[...], groups, table)
    u_one = (k_ref[...].astype(F32) * v_ref[...].astype(F32)).astype(BF16)
    extended = jnp.concatenate([halo_ref[...], u_one], axis=0)
    right = jnp.concatenate(
        [extended[b * taps : (b + 2) * taps] for b in range(blocks)], axis=1
    )
    product = jnp.dot(table[...], right, preferred_element_type=F32)
    lane_group = lax.broadcasted_iota(jnp.int32, (taps, LANES), 1) // width

    @pl.when(pl.program_id(0) == 0)
    def _():
        sq_ref[...] = jnp.zeros_like(sq_ref)

    for b in range(blocks):
        conv = product[:taps, b * LANES : (b + 1) * LANES]
        for g in range(1, groups):
            piece = product[g * taps : (g + 1) * taps, b * LANES : (b + 1) * LANES]
            conv = jnp.where(lane_group == g, piece, conv)
        rows = slice(b * taps, (b + 1) * taps)
        z = q_ref[rows, :].astype(F32) * conv
        z_ref[rows, :] = z
        sq_ref[rows, :] += z * z


def closing_kernel(z_ref, k_ref, sq_ref, gain_ref, rate_ref, u_ref, prior_ref, state_ref, u_wide):
    length = z_ref.shape[0]
    modes = rate_ref.shape[0]
    steps = length // SEGS
    scale = lax.rsqrt(sq_ref[...] / D + 1e-06)
    scaled = z_ref[...] * scale * gain_ref[...]
    u_two = (k_ref[...].astype(F32) * scaled).astype(BF16)
    u_ref[...] = u_two
    u_wide[...] = u_two.astype(F32)
    rates = rate_ref[...]
    decay = [
        jnp.broadcast_to(jnp.exp(-rates[m : m + 1, :]), (SEGS, LANES)) for m in range(modes)
    ]

    def step(t, states):
        x = u_wide[pl.ds(t, SEGS, stride=steps), :]
        return tuple(decay[m] * states[m] + x for m in range(modes))

    zero = jnp.zeros((SEGS, LANES), F32)
    states = lax.fori_loop(0, steps, step, (zero,) * modes, unroll=4)
    segment = lax.broadcasted_iota(jnp.int32, (SEGS, LANES), 0)
    for m in range(modes):
        total = states[m]
        shift = 1
        while shift < SEGS:
            factor = jnp.exp(-rates[m : m + 1, :] * (steps * shift))
            moved = jnp.where(segment >= shift, pltpu.roll(total, shift, 0), 0.0)
            total = total + factor * moved
            shift *= 2
        prior_ref[m * SEGS : (m + 1) * SEGS, :] = jnp.where(
            segment >= 1, pltpu.roll(total, 1, 0), 0.0
        )
        state_ref[m : m + 1, :] = total[SEGS - 1 :, :]


def modal_kernel(u_ref, q_ref, prior_ref, incoming_ref, rate_ref, weight_ref, out_ref, u_wide, y_wide):
    length = u_ref.shape[0]
    modes = rate_ref.shape[0]
    steps = length // SEGS
    u_wide[...] = u_ref[...].astype(F32)
    rates = rate_ref[...]
    decay = [
        jnp.broadcast_to(jnp.exp(-rates[m : m + 1, :]), (SEGS, LANES)) for m in range(modes)
    ]
    weight = [jnp.broadcast_to(weight_ref[m : m + 1, :], (SEGS, LANES)) for m in range(modes)]
    span = (lax.broadcasted_iota(jnp.int32, (SEGS, LANES), 0) * steps).astype(F32)
    states = tuple(
        prior_ref[m * SEGS : (m + 1) * SEGS, :]
        + jnp.exp(-rates[m : m + 1, :] * span) * incoming_ref[m : m + 1, :]
        for m in range(modes)
    )

    def step(t, states):
        rows = pl.ds(t, SEGS, stride=steps)
        x = u_wide[rows, :]
        states = tuple(decay[m] * states[m] + x for m in range(modes))
        terms = [weight[m] * states[m] for m in range(modes)]
        while len(terms) > 1:
            terms = [a + b for a, b in zip(terms[::2], terms[1::2])]
        y_wide[rows, :] = terms[0]
        return states

    lax.fori_loop(0, steps, step, states, unroll=4)
    out_ref[...] = (q_ref[...].astype(F32) * y_wide[...]).astype(BF16)


def on_device(q_one, k_one, v_one, mr_filter, norm_gain, q_two, k_two, li_rates, li_residues):
    length, channels = q_one.shape
    filters, taps = mr_filter.shape
    modes = li_rates.shape[0]
    devices = lax.axis_size("ctx")
    chunks = channels // LANES
    groups = filters // chunks
    tail = slice(length - taps, length)
    last = (k_one[tail].astype(F32) * v_one[tail].astype(F32)).astype(BF16)
    halo = lax.ppermute(last, "ctx", [(i, i + 1) for i in range(devices - 1)])
    mirrored = jnp.concatenate([mr_filter[:, :1], mr_filter[:, :0:-1]], axis=1).astype(F32)

    def tall(rows):
        return pl.BlockSpec((rows, LANES), lambda i: (0, i))

    def fixed(rows, columns):
        return pl.BlockSpec((rows, columns), lambda i: (0, 0))

    z, sq = pl.pallas_call(
        conv_kernel,
        grid=(chunks,),
        in_specs=[tall(length), tall(length), tall(length), tall(taps),
                  pl.BlockSpec((groups, taps), lambda i: (i, 0))],
        out_specs=[tall(length), fixed(length, LANES)],
        out_shape=[jax.ShapeDtypeStruct((length, channels), F32),
                   jax.ShapeDtypeStruct((length, LANES), F32)],
        scratch_shapes=[pltpu.VMEM((groups * taps, 2 * taps), BF16)],
        compiler_params=pltpu.CompilerParams(vmem_limit_bytes=40 << 20),
    )(q_one, k_one, v_one, halo, mirrored)
    squares = lax.psum(jnp.sum(sq, axis=1, keepdims=True), "tp")
    u_two, prior, closing = pl.pallas_call(
        closing_kernel,
        grid=(chunks,),
        in_specs=[tall(length), tall(length), fixed(length, 1), tall(1), tall(modes)],
        out_specs=[tall(length), tall(modes * SEGS), tall(modes)],
        out_shape=[jax.ShapeDtypeStruct((length, channels), BF16),
                   jax.ShapeDtypeStruct((modes * SEGS, channels), F32),
                   jax.ShapeDtypeStruct((modes, channels), F32)],
        scratch_shapes=[pltpu.VMEM((length, LANES), F32)],
        compiler_params=pltpu.CompilerParams(vmem_limit_bytes=40 << 20),
    )(z, k_two, squares, norm_gain[None, :], li_rates)
    own = channels // devices
    gathered = lax.all_to_all(closing, "ctx", split_axis=1, concat_axis=0, tiled=True)
    gathered = gathered.reshape(devices, modes, own)
    rates = lax.dynamic_slice_in_dim(li_rates, lax.axis_index("ctx") * own, own, 1)
    stride = jnp.exp(-rates * length)
    running = jnp.zeros((modes, own), F32)
    entering = []
    for d in range(devices):
        entering.append(running)
        running = stride * running + gathered[d]
    incoming = lax.all_to_all(
        jnp.concatenate(entering, axis=0), "ctx", split_axis=0, concat_axis=1, tiled=True
    )
    weights = li_residues * jnp.sqrt(-jnp.expm1(-2.0 * li_rates))
    return pl.pallas_call(
        modal_kernel,
        grid=(chunks,),
        in_specs=[tall(length), tall(length), tall(modes * SEGS), tall(modes), tall(modes), tall(modes)],
        out_specs=tall(length),
        out_shape=jax.ShapeDtypeStruct((length, channels), BF16),
        scratch_shapes=[pltpu.VMEM((length, LANES), F32), pltpu.VMEM((length, LANES), F32)],
        compiler_params=pltpu.CompilerParams(vmem_limit_bytes=40 << 20),
    )(u_two, q_two, prior, incoming, li_rates, weights)


def solution(mesh):
    in_specs = (
        P("ctx", "tp"),
        P("ctx", "tp"),
        P("ctx", "tp"),
        P("tp", None),
        P("tp"),
        P("ctx", "tp"),
        P("ctx", "tp"),
        P(None, "tp"),
        P(None, "tp"),
    )
    out_specs = P("ctx", "tp")
    return jax.shard_map(
        on_device, mesh=mesh, in_specs=in_specs, out_specs=out_specs, check_vma=False
    )
```

```python
import functools
import jax
import jax.numpy as jnp
from jax import lax
from jax.experimental import pallas as pl
from jax.experimental.pallas import tpu as pltpu
from jax.sharding import PartitionSpec as P

D = 8192
LANES = 128
SEGS = 8
F32 = jnp.float32
BF16 = jnp.bfloat16
MESH = pl.DeviceIdType.MESH
PIECES = 4


def toeplitz_rows(tap_rows, groups, earlier_store, own_store):
    taps = tap_rows.shape[1]
    row = lax.broadcasted_iota(jnp.int32, (taps, taps), 0)
    col = lax.broadcasted_iota(jnp.int32, (taps, taps), 1)
    later = col > row
    for g in range(groups):
        base = jnp.broadcast_to(tap_rows[g : g + 1, :], (8, taps))
        base = pltpu.roll(base, 0, 1, stride=1, stride_axis=0)
        tiles = [base if i == 0 else pltpu.roll(base, 8 * i, 1) for i in range(taps // 8)]
        circulant = jnp.concatenate(tiles, axis=0)
        rows = slice(g * taps, (g + 1) * taps)
        earlier_store[rows, :] = jnp.where(later, circulant, 0.0).astype(BF16)
        own_store[rows, :] = jnp.where(later, 0.0, circulant).astype(BF16)


def pick_groups(product, groups, taps):
    lane_group = lax.broadcasted_iota(jnp.int32, (taps, LANES), 1) // (LANES // groups)
    picked = product[:taps]
    for g in range(1, groups):
        picked = jnp.where(lane_group == g, product[g * taps : (g + 1) * taps], picked)
    return picked


def whole_kernel(
    ctx_size, tp_size, owners,
    q1_hbm, k1_hbm, v1_hbm, q2_hbm, k2_hbm, tap_ref, gain_ref, rate_ref, weight_ref,
    out_hbm,
    q1, k1, v1, q2, k2, out, u_one, halo, z, early, own_table, taps_f,
    squares, scale, u_wide, y_wide, prior, state, inbox, outbox, incoming,
    load_sem, halo_send, halo_recv, sq_send, sq_recv, in_send, in_recv, back_send, back_recv, out_sem,
):
    me = lax.axis_index("ctx")
    core = lax.axis_index("tp")
    length, channels = q1.shape
    filters, taps = tap_ref.shape
    modes = rate_ref.shape[0]
    chunks = channels // LANES
    groups = filters // chunks
    steps = length // SEGS
    own = channels // owners
    per_owner = own // LANES
    piece_width = channels // PIECES
    first, second = slice(0, taps), slice(taps, 2 * taps)

    barrier = pltpu.get_barrier_semaphore()

    @pl.loop(1, ctx_size)
    def _(k):
        pl.semaphore_signal(barrier, inc=1, device_id={"ctx": lax.rem(me + k, ctx_size)}, device_id_type=MESH)

    @pl.loop(1, tp_size)
    def _(k):
        pl.semaphore_signal(barrier, inc=1, device_id={"tp": lax.rem(core + k, tp_size)}, device_id_type=MESH)

    loads = [
        pltpu.make_async_copy(src.at[rows], dst.at[rows], load_sem.at[i])
        for i, (src, dst, rows) in enumerate([
            (k1_hbm, k1, pl.ds(taps, taps)), (v1_hbm, v1, pl.ds(taps, taps)),
            (k1_hbm, k1, pl.ds(0, taps)), (v1_hbm, v1, pl.ds(0, taps)),
            (q1_hbm, q1, pl.ds(0, length)), (k2_hbm, k2, pl.ds(0, length)),
            (q2_hbm, q2, pl.ds(0, length)),
        ])
    ]
    for load in loads:
        load.start()

    source = lax.broadcasted_iota(jnp.int32, (taps, taps), 0)
    target = lax.broadcasted_iota(jnp.int32, (taps, taps), 1)
    mirror = jnp.where(lax.rem(source + target, taps) == 0, 1.0, 0.0).astype(BF16)
    taps_f[...] = jnp.dot(tap_ref[...], mirror, preferred_element_type=F32)
    squares[core] = jnp.zeros((length, LANES), F32)

    def lanes_of(c):
        return pl.ds(pl.multiple_of(c * LANES, LANES), LANES)

    def gate(rows):
        @pl.loop(0, chunks)
        def _(c):
            at = lanes_of(c)
            u_one[rows, at] = (k1[rows, at].astype(F32) * v1[rows, at].astype(F32)).astype(BF16)

    loads[0].wait()
    loads[1].wait()
    gate(second)
    pl.semaphore_wait(barrier, ctx_size - 1 + tp_size - 1)

    def halo_copy(p):
        cols = pl.ds(p * piece_width, piece_width)
        return pltpu.make_async_remote_copy(
            src_ref=u_one.at[pl.ds(taps, taps), cols], dst_ref=halo.at[:, cols],
            send_sem=halo_send.at[p], recv_sem=halo_recv.at[p],
            device_id={"ctx": lax.rem(me + 1, ctx_size)}, device_id_type=MESH,
        )

    @pl.when(me < ctx_size - 1)
    def _():
        for p in range(PIECES):
            halo_copy(p).start()

    @pl.when(me == 0)
    def _():
        halo[...] = jnp.zeros_like(halo)

    loads[2].wait()
    loads[3].wait()
    gate(first)
    loads[4].wait()

    @pl.loop(0, chunks)
    def _(c):
        at = lanes_of(c)
        tap_rows = taps_f[pl.ds(pl.multiple_of(c * groups, groups), groups), :]
        toeplitz_rows(tap_rows, groups, early.at[c], own_table)
        left = jnp.concatenate([early[c], own_table[...]], axis=1)
        head, rest = u_one[first, at], u_one[second, at]
        right = jnp.concatenate([
            jnp.concatenate([jnp.zeros_like(head), head], axis=0),
            jnp.concatenate([head, rest], axis=0),
        ], axis=1)
        product = jnp.dot(left, right, preferred_element_type=F32)
        z[first, at] = pick_groups(product[:, :LANES], groups, taps)
        late = q1[second, at].astype(F32) * pick_groups(product[:, LANES:], groups, taps)
        z[second, at] = late
        squares[core, second, :] += late * late

    pairs = chunks // PIECES // 2
    for p in range(PIECES):
        @pl.when(me > 0)
        def _():
            halo_copy(p).wait_recv()

        @pl.loop(p * pairs, (p + 1) * pairs)
        def _(pair):
            left = jnp.concatenate([early[2 * pair], early[2 * pair + 1]], axis=1)
            one, two = halo[:, lanes_of(2 * pair)], halo[:, lanes_of(2 * pair + 1)]
            zero = jnp.zeros_like(one)
            right = jnp.concatenate([
                jnp.concatenate([one, zero], axis=0), jnp.concatenate([zero, two], axis=0)
            ], axis=1)
            product = jnp.dot(left, right, preferred_element_type=F32)
            for i in range(2):
                at = lanes_of(2 * pair + i)
                conv = z[first, at] + pick_groups(product[:, i * LANES : (i + 1) * LANES], groups, taps)
                value = q1[first, at].astype(F32) * conv
                z[first, at] = value
                squares[core, first, :] += value * value

    def square_copy(k, slot):
        return pltpu.make_async_remote_copy(
            src_ref=squares.at[core], dst_ref=squares.at[slot],
            send_sem=sq_send.at[k], recv_sem=sq_recv.at[slot],
            device_id={"tp": lax.rem(core + k, tp_size)}, device_id_type=MESH,
        )

    @pl.loop(1, tp_size)
    def _(k):
        square_copy(k, core).start()

    loads[5].wait()

    @pl.loop(1, tp_size)
    def _(k):
        square_copy(k, lax.rem(core + k, tp_size)).wait_recv()

    total = squares[0]
    for i in range(1, tp_size):
        total = total + squares[i]
    total = jnp.sum(total, axis=1, keepdims=True)
    scale[...] = jnp.broadcast_to(lax.rsqrt(total / D + 1e-06), (length, LANES))

    segment = lax.broadcasted_iota(jnp.int32, (SEGS, LANES), 0)

    def decays(at):
        return [jnp.broadcast_to(jnp.exp(-rate_ref[m : m + 1, at]), (SEGS, LANES)) for m in range(modes)]

    def in_copy(j):
        return pltpu.make_async_remote_copy(
            src_ref=state.at[j], dst_ref=inbox.at[me],
            send_sem=in_send.at[j], recv_sem=in_recv.at[me],
            device_id={"ctx": j}, device_id_type=MESH,
        )

    @pl.loop(0, owners)
    def _(k):
        j = lax.rem(me + 1 + k, owners)
        for i in range(per_owner):
            at = lanes_of(j * per_owner + i)
            scaled = z[:, at] * scale[...] * gain_ref[:, at]
            u_two = (k2[:, at].astype(F32) * scaled).astype(BF16).astype(F32)
            z[:, at] = u_two
            u_wide[i] = u_two
            decay = decays(at)

            def step(t, states):
                x = u_wide[i, pl.ds(t, SEGS, stride=steps), :]
                return tuple(decay[m] * states[m] + x for m in range(modes))

            states = lax.fori_loop(
                0, steps, step, (jnp.zeros((SEGS, LANES), F32),) * modes, unroll=8
            )
            for m in range(modes):
                inclusive = states[m]
                shift = 1
                while shift < SEGS:
                    factor = jnp.exp(-rate_ref[m : m + 1, at] * (steps * shift))
                    moved = jnp.where(segment >= shift, pltpu.roll(inclusive, shift, 0), 0.0)
                    inclusive = inclusive + factor * moved
                    shift *= 2
                prior[m * SEGS : (m + 1) * SEGS, at] = jnp.where(
                    segment >= 1, pltpu.roll(inclusive, 1, 0), 0.0
                )
                state[j, m : m + 1, i * LANES : (i + 1) * LANES] = inclusive[SEGS - 1 :, :]

        @pl.when(j != me)
        def _():
            in_copy(j).start()

    def in_arrival(d):
        return pltpu.make_async_remote_copy(
            src_ref=state.at[0], dst_ref=inbox.at[d],
            send_sem=in_send.at[0], recv_sem=in_recv.at[d],
            device_id={"ctx": d}, device_id_type=MESH,
        )

    def back_copy(d):
        return pltpu.make_async_remote_copy(
            src_ref=outbox.at[d], dst_ref=incoming.at[me],
            send_sem=back_send.at[d], recv_sem=back_recv.at[me],
            device_id={"ctx": d}, device_id_type=MESH,
        )

    def back_arrival(j):
        return pltpu.make_async_remote_copy(
            src_ref=outbox.at[0], dst_ref=incoming.at[j],
            send_sem=back_send.at[0], recv_sem=back_recv.at[j],
            device_id={"ctx": j}, device_id_type=MESH,
        )

    @pl.when(me < owners)
    def _():
        inbox[me] = state[lax.rem(me, owners)]
        mine = pl.ds(pl.multiple_of(lax.rem(me, owners) * own, own), own)
        stride = jnp.exp(-rate_ref[:, mine] * length)

        def pass_on(d, running):
            @pl.when(d != me)
            def _():
                in_arrival(d).wait_recv()
            outbox[d] = running

            @pl.when(d != me)
            def _():
                back_copy(d).start()

            @pl.when(d == me)
            def _():
                incoming[lax.rem(me, owners)] = running
            return stride * running + inbox[d]

        lax.fori_loop(0, ctx_size, pass_on, jnp.zeros((modes, own), F32))

    loads[6].wait()
    span = (segment * steps).astype(F32)

    def out_copy(j):
        cols = pl.ds(pl.multiple_of(j * own, own), own)
        return pltpu.make_async_copy(out.at[:, cols], out_hbm.at[:, cols], out_sem.at[j])

    @pl.loop(0, owners)
    def _(j):
        @pl.when(j != me)
        def _():
            back_arrival(j).wait_recv()
        for i in range(per_owner):
            at = lanes_of(j * per_owner + i)
            u_wide[i] = z[:, at]
            decay = decays(at)
            weight = [jnp.broadcast_to(weight_ref[m : m + 1, at], (SEGS, LANES)) for m in range(modes)]
            states = tuple(
                prior[m * SEGS : (m + 1) * SEGS, at]
                + jnp.exp(-rate_ref[m : m + 1, at] * span)
                * incoming[j, m : m + 1, i * LANES : (i + 1) * LANES]
                for m in range(modes)
            )

            def step(t, states):
                rows = pl.ds(t, SEGS, stride=steps)
                x = u_wide[i, rows, :]
                states = tuple(decay[m] * states[m] + x for m in range(modes))
                terms = [weight[m] * states[m] for m in range(modes)]
                while len(terms) > 1:
                    terms = [a + b for a, b in zip(terms[::2], terms[1::2])]
                y_wide[i, rows, :] = terms[0]
                return states

            lax.fori_loop(0, steps, step, states, unroll=8)
            out[:, at] = (q2[:, at].astype(F32) * y_wide[i]).astype(BF16)
        out_copy(j).start()

    @pl.loop(0, owners)
    def _(j):
        out_copy(j).wait()

        @pl.when(j != me)
        def _():
            in_copy(j).wait_send()

    @pl.when(me < owners)
    def _():
        @pl.loop(0, ctx_size)
        def _(d):
            @pl.when(d != me)
            def _():
                back_copy(d).wait_send()

    @pl.loop(1, tp_size)
    def _(k):
        square_copy(k, core).wait_send()

    @pl.when(me < ctx_size - 1)
    def _():
        for p in range(PIECES):
            halo_copy(p).wait_send()


def on_device(q_one, k_one, v_one, mr_filter, norm_gain, q_two, k_two, li_rates, li_residues):
    length, channels = q_one.shape
    filters, taps = mr_filter.shape
    modes = li_rates.shape[0]
    ctx_size, tp_size = lax.axis_size("ctx"), lax.axis_size("tp")
    owners = min(ctx_size, channels // LANES)
    own = channels // owners
    chunks = channels // LANES
    table_rows = filters // chunks * taps
    weights = li_residues * jnp.sqrt(-jnp.expm1(-2.0 * li_rates))
    wide = pltpu.VMEM((length, channels), BF16)
    dma = pltpu.SemaphoreType.DMA
    anywhere = pl.BlockSpec(memory_space=pl.ANY)
    inside = pl.BlockSpec(memory_space=pltpu.VMEM)
    return pl.pallas_call(
        functools.partial(whole_kernel, ctx_size, tp_size, owners),
        in_specs=[anywhere] * 5 + [inside] * 4,
        out_specs=anywhere,
        out_shape=jax.ShapeDtypeStruct((length, channels), BF16),
        scratch_shapes=[
            wide, wide, wide, wide, wide, wide, wide,
            pltpu.VMEM((taps, channels), BF16),
            pltpu.VMEM((length, channels), F32),
            pltpu.VMEM((chunks, table_rows, taps), BF16),
            pltpu.VMEM((table_rows, taps), BF16),
            pltpu.VMEM((filters, taps), F32),
            pltpu.VMEM((tp_size, length, LANES), F32),
            pltpu.VMEM((length, LANES), F32),
            pltpu.VMEM((own // LANES, length, LANES), F32),
            pltpu.VMEM((own // LANES, length, LANES), F32),
            pltpu.VMEM((modes * SEGS, channels), F32),
            pltpu.VMEM((owners, modes, own), F32),
            pltpu.VMEM((ctx_size, modes, own), F32),
            pltpu.VMEM((ctx_size, modes, own), F32),
            pltpu.VMEM((owners, modes, own), F32),
            dma((7,)), dma((PIECES,)), dma((PIECES,)), dma((tp_size,)), dma((tp_size,)),
            dma((owners,)), dma((ctx_size,)), dma((ctx_size,)), dma((owners,)), dma((owners,)),
        ],
        compiler_params=pltpu.CompilerParams(
            vmem_limit_bytes=60 << 20, collective_id=0, has_side_effects=True
        ),
    )(q_one, k_one, v_one, q_two, k_two, mr_filter, norm_gain[None, :], li_rates, weights)


def solution(mesh):
    in_specs = (
        P("ctx", "tp"),
        P("ctx", "tp"),
        P("ctx", "tp"),
        P("tp", None),
        P("tp"),
        P("ctx", "tp"),
        P("ctx", "tp"),
        P(None, "tp"),
        P(None, "tp"),
    )
    out_specs = P("ctx", "tp")
    return jax.shard_map(
        on_device, mesh=mesh, in_specs=in_specs, out_specs=out_specs, check_vma=False
    )
```

```python
import functools
import jax
import jax.numpy as jnp
from jax import lax
from jax.experimental import pallas as pl
from jax.experimental.pallas import tpu as pltpu
from jax.sharding import PartitionSpec as P

D = 8192
LANES = 128
SEGS = 8
F32 = jnp.float32
BF16 = jnp.bfloat16
MESH = pl.DeviceIdType.MESH
PIECES = 4


def toeplitz_rows(tap_rows, groups, earlier_store, own_store):
    taps = tap_rows.shape[1]
    row = lax.broadcasted_iota(jnp.int32, (taps, taps), 0)
    col = lax.broadcasted_iota(jnp.int32, (taps, taps), 1)
    later = col > row
    for g in range(groups):
        base = jnp.broadcast_to(tap_rows[g : g + 1, :], (8, taps))
        base = pltpu.roll(base, 0, 1, stride=1, stride_axis=0)
        tiles = [base if i == 0 else pltpu.roll(base, 8 * i, 1) for i in range(taps // 8)]
        circulant = jnp.concatenate(tiles, axis=0)
        rows = slice(g * taps, (g + 1) * taps)
        earlier_store[rows, :] = jnp.where(later, circulant, 0.0).astype(BF16)
        own_store[rows, :] = jnp.where(later, 0.0, circulant).astype(BF16)


def pick_groups(product, groups, taps):
    lane_group = lax.broadcasted_iota(jnp.int32, (taps, LANES), 1) // (LANES // groups)
    picked = product[:taps]
    for g in range(1, groups):
        picked = jnp.where(lane_group == g, product[g * taps : (g + 1) * taps], picked)
    return picked


def whole_kernel(
    ctx_size, tp_size, owners,
    q1_hbm, k1_hbm, v1_hbm, q2_hbm, k2_hbm, tap_ref, gain_ref, rate_ref, residue_ref,
    out_hbm,
    q1, k1, v1, q2, k2, out, u_one, halo, z, early, own_table, taps_f,
    squares, scale, u_wide, y_wide, y, weights, prior, early_state, late_state, closing,
    state, inbox, outbox, incoming,
    load_sem, halo_send, halo_recv, sq_send, sq_recv, in_send, in_recv, back_send, back_recv, out_sem,
):
    me = lax.axis_index("ctx")
    core = lax.axis_index("tp")
    length, channels = q1.shape
    filters, taps = tap_ref.shape
    modes = rate_ref.shape[0]
    chunks = channels // LANES
    groups = filters // chunks
    steps = taps // SEGS
    own = channels // owners
    per_owner = own // LANES
    piece_width = channels // PIECES
    first, second = slice(0, taps), slice(taps, 2 * taps)

    barrier = pltpu.get_barrier_semaphore()

    @pl.loop(1, ctx_size)
    def _(k):
        pl.semaphore_signal(barrier, inc=1, device_id={"ctx": lax.rem(me + k, ctx_size)}, device_id_type=MESH)

    @pl.loop(1, tp_size)
    def _(k):
        pl.semaphore_signal(barrier, inc=1, device_id={"tp": lax.rem(core + k, tp_size)}, device_id_type=MESH)

    loads = [
        pltpu.make_async_copy(src.at[rows], dst.at[rows], load_sem.at[i])
        for i, (src, dst, rows) in enumerate([
            (k1_hbm, k1, pl.ds(taps, taps)), (v1_hbm, v1, pl.ds(taps, taps)),
            (k1_hbm, k1, pl.ds(0, taps)), (v1_hbm, v1, pl.ds(0, taps)),
            (q1_hbm, q1, pl.ds(0, length)), (k2_hbm, k2, pl.ds(0, length)),
            (q2_hbm, q2, pl.ds(0, length)),
        ])
    ]
    for load in loads:
        load.start()

    source = lax.broadcasted_iota(jnp.int32, (taps, taps), 0)
    target = lax.broadcasted_iota(jnp.int32, (taps, taps), 1)
    mirror = jnp.where(lax.rem(source + target, taps) == 0, 1.0, 0.0).astype(BF16)
    taps_f[...] = jnp.dot(tap_ref[...], mirror, preferred_element_type=F32)
    squares[core] = jnp.zeros((length, LANES), F32)

    def lanes_of(c):
        return pl.ds(pl.multiple_of(c * LANES, LANES), LANES)

    def gate(rows):
        @pl.loop(0, chunks)
        def _(c):
            at = lanes_of(c)
            u_one[rows, at] = (k1[rows, at].astype(F32) * v1[rows, at].astype(F32)).astype(BF16)

    loads[0].wait()
    loads[1].wait()
    gate(second)
    pl.semaphore_wait(barrier, ctx_size - 1 + tp_size - 1)

    def halo_copy(p):
        cols = pl.ds(p * piece_width, piece_width)
        return pltpu.make_async_remote_copy(
            src_ref=u_one.at[pl.ds(taps, taps), cols], dst_ref=halo.at[:, cols],
            send_sem=halo_send.at[p], recv_sem=halo_recv.at[p],
            device_id={"ctx": lax.rem(me + 1, ctx_size)}, device_id_type=MESH,
        )

    @pl.when(me < ctx_size - 1)
    def _():
        for p in range(PIECES):
            halo_copy(p).start()

    @pl.when(me == 0)
    def _():
        halo[...] = jnp.zeros_like(halo)

    loads[2].wait()
    loads[3].wait()
    gate(first)
    loads[4].wait()

    @pl.loop(0, chunks)
    def _(c):
        at = lanes_of(c)
        tap_rows = taps_f[pl.ds(pl.multiple_of(c * groups, groups), groups), :]
        toeplitz_rows(tap_rows, groups, early.at[c], own_table)
        left = jnp.concatenate([early[c], own_table[...]], axis=1)
        head, rest = u_one[first, at], u_one[second, at]
        right = jnp.concatenate([
            jnp.concatenate([jnp.zeros_like(head), head], axis=0),
            jnp.concatenate([head, rest], axis=0),
        ], axis=1)
        product = jnp.dot(left, right, preferred_element_type=F32)
        z[first, at] = pick_groups(product[:, :LANES], groups, taps)
        late = q1[second, at].astype(F32) * pick_groups(product[:, LANES:], groups, taps)
        z[second, at] = late
        squares[core, second, :] += late * late

    segment = lax.broadcasted_iota(jnp.int32, (SEGS, LANES), 0)
    span = (segment * steps).astype(F32)
    halves = (first, second)

    def square_copy(h, k, slot):
        rows = pl.ds(h * taps, taps)
        return pltpu.make_async_remote_copy(
            src_ref=squares.at[core, rows], dst_ref=squares.at[slot, rows],
            send_sem=sq_send.at[h, k], recv_sem=sq_recv.at[h, slot],
            device_id={"tp": lax.rem(core + k, tp_size)}, device_id_type=MESH,
        )

    def send_squares(h):
        @pl.loop(1, tp_size)
        def _(k):
            square_copy(h, k, core).start()

    def find_scale(h):
        @pl.loop(1, tp_size)
        def _(k):
            square_copy(h, k, lax.rem(core + k, tp_size)).wait_recv()
        total = squares[0, halves[h], :]
        for i in range(1, tp_size):
            total = total + squares[i, halves[h], :]
        total = jnp.sum(total, axis=1, keepdims=True)
        scale[halves[h], :] = jnp.broadcast_to(lax.rsqrt(total / D + 1e-06), (taps, LANES))

    def decays(at):
        return [jnp.broadcast_to(jnp.exp(-rate_ref[m : m + 1, at]), (SEGS, LANES)) for m in range(modes)]

    def set_signal(h, at, i):
        scaled = z[halves[h], at] * scale[halves[h], :] * gain_ref[:, at]
        u_two = (k2[halves[h], at].astype(F32) * scaled).astype(BF16).astype(F32)
        z[halves[h], at] = u_two
        u_wide[i] = u_two

    zero_states = (jnp.zeros((SEGS, LANES), F32),) * modes

    def local_pass(h, at, i):
        decay = decays(at)
        weight = [jnp.broadcast_to(weights[m : m + 1, at], (SEGS, LANES)) for m in range(modes)]

        def step(t, states):
            rows = pl.ds(t, SEGS, stride=steps)
            x = u_wide[i, rows, :]
            states = tuple(decay[m] * states[m] + x for m in range(modes))
            terms = [weight[m] * states[m] for m in range(modes)]
            while len(terms) > 1:
                terms = [a + b for a, b in zip(terms[::2], terms[1::2])]
            y_wide[i, rows, :] = terms[0]
            return states

        states = lax.fori_loop(0, steps, step, zero_states, unroll=8)
        y[halves[h], at] = y_wide[i, :taps, :]
        return states

    def closing_pass(at, i):
        decay = decays(at)

        def step(t, states):
            x = u_wide[i, pl.ds(t, SEGS, stride=steps), :]
            return tuple(decay[m] * states[m] + x for m in range(modes))

        return lax.fori_loop(0, steps, step, zero_states, unroll=16)

    def join_segments(h, at, m, inclusive):
        factor = jnp.exp(-rate_ref[m : m + 1, at] * steps)
        shift = 1
        while shift < SEGS:
            moved = jnp.where(segment >= shift, pltpu.roll(inclusive, shift, 0), 0.0)
            inclusive = inclusive + factor * moved
            factor = factor * factor
            shift *= 2
        prior[h, m * SEGS : (m + 1) * SEGS, at] = jnp.where(
            segment >= 1, pltpu.roll(inclusive, 1, 0), 0.0
        )
        return inclusive[SEGS - 1 :, :], factor

    send_squares(1)

    @pl.loop(0, chunks)
    def _(c):
        at = lanes_of(c)
        double = 2.0 * rate_ref[:, at]
        series = jnp.ones_like(double)
        for order in range(10, 1, -1):
            series = 1.0 - double * series * (1.0 / order)
        gap = jnp.where(double < 0.5, double * series, 1.0 - jnp.exp(-double))
        weights[:, at] = residue_ref[:, at] * jnp.sqrt(gap)

    loads[5].wait()
    find_scale(1)

    @pl.loop(0, chunks // 2)
    def _(pair):
        for i in range(2):
            at = lanes_of(2 * pair + i)
            set_signal(1, at, i)
            states = local_pass(1, at, i)
            for m in range(modes):
                last, _ = join_segments(1, at, m, states[m])
                late_state[m : m + 1, at] = last

    pairs = chunks // PIECES // 2
    for p in range(PIECES):
        @pl.when(me > 0)
        def _():
            halo_copy(p).wait_recv()

        @pl.loop(p * pairs, (p + 1) * pairs)
        def _(pair):
            left = jnp.concatenate([early[2 * pair], early[2 * pair + 1]], axis=1)
            one, two = halo[:, lanes_of(2 * pair)], halo[:, lanes_of(2 * pair + 1)]
            zero = jnp.zeros_like(one)
            right = jnp.concatenate([
                jnp.concatenate([one, zero], axis=0), jnp.concatenate([zero, two], axis=0)
            ], axis=1)
            product = jnp.dot(left, right, preferred_element_type=F32)
            for i in range(2):
                at = lanes_of(2 * pair + i)
                conv = z[first, at] + pick_groups(product[:, i * LANES : (i + 1) * LANES], groups, taps)
                value = q1[first, at].astype(F32) * conv
                z[first, at] = value
                squares[core, first, :] += value * value

    send_squares(0)
    find_scale(0)

    def in_copy(j):
        return pltpu.make_async_remote_copy(
            src_ref=state.at[j], dst_ref=inbox.at[me],
            send_sem=in_send.at[j], recv_sem=in_recv.at[me],
            device_id={"ctx": j}, device_id_type=MESH,
        )

    @pl.loop(0, owners)
    def _(k):
        j = lax.rem(me + 1 + k, owners)
        for i in range(per_owner):
            at = lanes_of(j * per_owner + i)
            set_signal(0, at, i)
            states = closing_pass(at, i)
            for m in range(modes):
                last, factor = join_segments(0, at, m, states[m])
                early_state[m : m + 1, at] = last
                closing[m : m + 1, :] = factor * last + late_state[m : m + 1, at]
            state[j, :, i * LANES : (i + 1) * LANES] = closing[...].astype(BF16)

        @pl.when(j != me)
        def _():
            in_copy(j).start()

    def local_first(start, stop):
        @pl.loop(start, stop)
        def _(pair):
            for i in range(2):
                at = lanes_of(2 * pair + i)
                u_wide[i] = z[first, at]
                local_pass(0, at, i)

    def in_arrival(d):
        return pltpu.make_async_remote_copy(
            src_ref=state.at[0], dst_ref=inbox.at[d],
            send_sem=in_send.at[0], recv_sem=in_recv.at[d],
            device_id={"ctx": d}, device_id_type=MESH,
        )

    def back_copy(d):
        return pltpu.make_async_remote_copy(
            src_ref=outbox.at[d], dst_ref=incoming.at[me],
            send_sem=back_send.at[d], recv_sem=back_recv.at[me],
            device_id={"ctx": d}, device_id_type=MESH,
        )

    def back_arrival(j):
        return pltpu.make_async_remote_copy(
            src_ref=outbox.at[0], dst_ref=incoming.at[j],
            send_sem=back_send.at[0], recv_sem=back_recv.at[j],
            device_id={"ctx": j}, device_id_type=MESH,
        )

    early_pairs = chunks // 4
    local_first(0, early_pairs)

    @pl.when(me < owners)
    def _():
        inbox[me] = state[lax.rem(me, owners)]
        mine = pl.ds(pl.multiple_of(lax.rem(me, owners) * own, own), own)
        stride = jnp.exp(-rate_ref[:, mine] * length)

        def pass_on(d, running):
            @pl.when(d != me)
            def _():
                in_arrival(d).wait_recv()
            sent = running.astype(BF16)
            outbox[d] = sent

            @pl.when(d != me)
            def _():
                back_copy(d).start()

            @pl.when(d == me)
            def _():
                incoming[lax.rem(me, owners)] = sent
            return stride * running + inbox[d].astype(F32)

        lax.fori_loop(0, ctx_size, pass_on, jnp.zeros((modes, own), F32))

    local_first(early_pairs, chunks // 2)
    loads[6].wait()

    def out_copy(j):
        cols = pl.ds(pl.multiple_of(j * own, own), own)
        return pltpu.make_async_copy(out.at[:, cols], out_hbm.at[:, cols], out_sem.at[j])

    @pl.loop(0, owners)
    def _(j):
        @pl.when(j != me)
        def _():
            back_arrival(j).wait_recv()
        for i in range(per_owner):
            at = lanes_of(j * per_owner + i)
            decay = decays(at)
            entering = []
            for h in range(2):
                for m in range(modes):
                    rate = rate_ref[m : m + 1, at]
                    arrived = incoming[j, m : m + 1, i * LANES : (i + 1) * LANES].astype(F32)
                    if h == 1:
                        arrived = early_state[m : m + 1, at] + jnp.exp(-rate * taps) * arrived
                    begin = prior[h, m * SEGS : (m + 1) * SEGS, at] + jnp.exp(-rate * span) * arrived
                    entering.append(weights[m : m + 1, at] * begin)

            def step(t, entering):
                entering = tuple(decay[m % modes] * entering[m] for m in range(2 * modes))
                for h in range(2):
                    terms = entering[h * modes : (h + 1) * modes]
                    while len(terms) > 1:
                        terms = [a + b for a, b in zip(terms[::2], terms[1::2])]
                    y_wide[i, pl.ds(h * taps + t, SEGS, stride=steps), :] = terms[0]
                return entering

            lax.fori_loop(0, steps, step, tuple(entering), unroll=8)
            out[:, at] = (q2[:, at].astype(F32) * (y[:, at] + y_wide[i])).astype(BF16)
        out_copy(j).start()

    @pl.loop(0, owners)
    def _(j):
        out_copy(j).wait()

        @pl.when(j != me)
        def _():
            in_copy(j).wait_send()

    @pl.when(me < owners)
    def _():
        @pl.loop(0, ctx_size)
        def _(d):
            @pl.when(d != me)
            def _():
                back_copy(d).wait_send()

    @pl.loop(1, tp_size)
    def _(k):
        square_copy(0, k, core).wait_send()
        square_copy(1, k, core).wait_send()

    @pl.when(me < ctx_size - 1)
    def _():
        for p in range(PIECES):
            halo_copy(p).wait_send()


def on_device(q_one, k_one, v_one, mr_filter, norm_gain, q_two, k_two, li_rates, li_residues):
    length, channels = q_one.shape
    filters, taps = mr_filter.shape
    modes = li_rates.shape[0]
    ctx_size, tp_size = lax.axis_size("ctx"), lax.axis_size("tp")
    owners = min(ctx_size, channels // LANES)
    own = channels // owners
    chunks = channels // LANES
    table_rows = filters // chunks * taps
    wide = pltpu.VMEM((length, channels), BF16)
    dma = pltpu.SemaphoreType.DMA
    anywhere = pl.BlockSpec(memory_space=pl.ANY)
    inside = pl.BlockSpec(memory_space=pltpu.VMEM)
    return pl.pallas_call(
        functools.partial(whole_kernel, ctx_size, tp_size, owners),
        in_specs=[anywhere] * 5 + [inside] * 4,
        out_specs=anywhere,
        out_shape=jax.ShapeDtypeStruct((length, channels), BF16),
        scratch_shapes=[
            wide, wide, wide, wide, wide, wide, wide,
            pltpu.VMEM((taps, channels), BF16),
            pltpu.VMEM((length, channels), F32),
            pltpu.VMEM((chunks, table_rows, taps), BF16),
            pltpu.VMEM((table_rows, taps), BF16),
            pltpu.VMEM((filters, taps), F32),
            pltpu.VMEM((tp_size, length, LANES), F32),
            pltpu.VMEM((length, LANES), F32),
            pltpu.VMEM((max(2, own // LANES), taps, LANES), F32),
            pltpu.VMEM((max(2, own // LANES), length, LANES), F32),
            pltpu.VMEM((length, channels), F32),
            pltpu.VMEM((modes, channels), F32),
            pltpu.VMEM((2, modes * SEGS, channels), F32),
            pltpu.VMEM((modes, channels), F32),
            pltpu.VMEM((modes, channels), F32),
            pltpu.VMEM((modes, LANES), F32),
            pltpu.VMEM((owners, modes, own), BF16),
            pltpu.VMEM((ctx_size, modes, own), BF16),
            pltpu.VMEM((ctx_size, modes, own), BF16),
            pltpu.VMEM((owners, modes, own), BF16),
            dma((7,)), dma((PIECES,)), dma((PIECES,)), dma((2, tp_size)), dma((2, tp_size)),
            dma((owners,)), dma((ctx_size,)), dma((ctx_size,)), dma((owners,)), dma((owners,)),
        ],
        compiler_params=pltpu.CompilerParams(
            vmem_limit_bytes=60 << 20, collective_id=0, has_side_effects=True
        ),
    )(q_one, k_one, v_one, q_two, k_two, mr_filter, norm_gain[None, :], li_rates, li_residues)


def solution(mesh):
    in_specs = (
        P("ctx", "tp"),
        P("ctx", "tp"),
        P("ctx", "tp"),
        P("tp", None),
        P("tp"),
        P("ctx", "tp"),
        P("ctx", "tp"),
        P(None, "tp"),
        P(None, "tp"),
    )
    out_specs = P("ctx", "tp")
    return jax.shard_map(
        on_device, mesh=mesh, in_specs=in_specs, out_specs=out_specs, check_vma=False
    )
```

```python
import functools
import jax
import jax.numpy as jnp
from jax import lax
from jax.experimental import pallas as pl
from jax.experimental.pallas import tpu as pltpu
from jax.sharding import PartitionSpec as P

D = 8192
LANES = 128
SEGS = 8
F32 = jnp.float32
BF16 = jnp.bfloat16
MESH = pl.DeviceIdType.MESH
PIECES = 4


def toeplitz_rows(tap_rows, groups, earlier_store, own_store):
    taps = tap_rows.shape[1]
    row = lax.broadcasted_iota(jnp.int32, (taps, taps), 0)
    col = lax.broadcasted_iota(jnp.int32, (taps, taps), 1)
    later = col > row
    for g in range(groups):
        base = jnp.broadcast_to(tap_rows[g : g + 1, :], (8, taps))
        base = pltpu.roll(base, 0, 1, stride=1, stride_axis=0)
        tiles = [base if i == 0 else pltpu.roll(base, 8 * i, 1) for i in range(taps // 8)]
        circulant = jnp.concatenate(tiles, axis=0)
        rows = slice(g * taps, (g + 1) * taps)
        earlier_store[rows, :] = jnp.where(later, circulant, 0.0).astype(BF16)
        own_store[rows, :] = jnp.where(later, 0.0, circulant).astype(BF16)


def pick_groups(product, groups, taps):
    lane_group = lax.broadcasted_iota(jnp.int32, (taps, LANES), 1) // (LANES // groups)
    picked = product[:taps]
    for g in range(1, groups):
        picked = jnp.where(lane_group == g, product[g * taps : (g + 1) * taps], picked)
    return picked


def whole_kernel(
    ctx_size, tp_size, owners,
    q1_hbm, k1_hbm, v1_hbm, q2_hbm, k2_hbm, tap_ref, gain_ref, rate_ref, residue_ref,
    out_hbm,
    q1, k1, v1, q2, k2, out, u_one, halo, z, early, own_table, taps_f,
    squares, scale, u_wide, y_wide, y, weights, prior, early_state, late_state,
    decay_one, decay_seg, decay_half,
    state, inbox, outbox, incoming,
    load_sem, halo_send, halo_recv, sq_send, sq_recv, in_send, in_recv, back_send, back_recv, out_sem,
):
    me = lax.axis_index("ctx")
    core = lax.axis_index("tp")
    length, channels = q1.shape
    filters, taps = tap_ref.shape
    modes = rate_ref.shape[0]
    chunks = channels // LANES
    groups = filters // chunks
    steps = taps // SEGS
    own = channels // owners
    per_owner = own // LANES
    piece_width = channels // PIECES
    first, second = slice(0, taps), slice(taps, 2 * taps)

    barrier = pltpu.get_barrier_semaphore()

    @pl.loop(1, ctx_size)
    def _(k):
        pl.semaphore_signal(barrier, inc=1, device_id={"ctx": lax.rem(me + k, ctx_size)}, device_id_type=MESH)

    @pl.loop(1, tp_size)
    def _(k):
        pl.semaphore_signal(barrier, inc=1, device_id={"tp": lax.rem(core + k, tp_size)}, device_id_type=MESH)

    loads = [
        pltpu.make_async_copy(src.at[rows], dst.at[rows], load_sem.at[i])
        for i, (src, dst, rows) in enumerate([
            (k1_hbm, k1, pl.ds(taps, taps)), (v1_hbm, v1, pl.ds(taps, taps)),
            (k1_hbm, k1, pl.ds(0, taps)), (v1_hbm, v1, pl.ds(0, taps)),
            (q1_hbm, q1, pl.ds(0, length)), (k2_hbm, k2, pl.ds(0, length)),
            (q2_hbm, q2, pl.ds(0, length)),
        ])
    ]
    for load in loads:
        load.start()

    source = lax.broadcasted_iota(jnp.int32, (taps, taps), 0)
    target = lax.broadcasted_iota(jnp.int32, (taps, taps), 1)
    mirror = jnp.where(lax.rem(source + target, taps) == 0, 1.0, 0.0).astype(BF16)
    taps_f[...] = jnp.dot(tap_ref[...], mirror, preferred_element_type=F32)
    squares[core] = jnp.zeros((length, LANES), F32)

    def lanes_of(c):
        return pl.ds(pl.multiple_of(c * LANES, LANES), LANES)

    def gate(rows):
        @pl.loop(0, chunks)
        def _(c):
            at = lanes_of(c)
            u_one[rows, at] = (k1[rows, at].astype(F32) * v1[rows, at].astype(F32)).astype(BF16)

    loads[0].wait()
    loads[1].wait()
    gate(second)
    pl.semaphore_wait(barrier, ctx_size - 1 + tp_size - 1)

    def halo_copy(p):
        cols = pl.ds(p * piece_width, piece_width)
        return pltpu.make_async_remote_copy(
            src_ref=u_one.at[pl.ds(taps, taps), cols], dst_ref=halo.at[:, cols],
            send_sem=halo_send.at[p], recv_sem=halo_recv.at[p],
            device_id={"ctx": lax.rem(me + 1, ctx_size)}, device_id_type=MESH,
        )

    @pl.when(me < ctx_size - 1)
    def _():
        for p in range(PIECES):
            halo_copy(p).start()

    @pl.when(me == 0)
    def _():
        halo[...] = jnp.zeros_like(halo)

    loads[2].wait()
    loads[3].wait()
    gate(first)
    loads[4].wait()

    def make_tables(c, slot):
        tap_rows = taps_f[pl.ds(pl.multiple_of(c * groups, groups), groups), :]
        toeplitz_rows(tap_rows, groups, early.at[c], own_table.at[slot])

    def main_product(c, slot):
        at = lanes_of(c)
        left = jnp.concatenate([early[c], own_table[slot]], axis=1)
        head, rest = u_one[first, at], u_one[second, at]
        right = jnp.concatenate([
            jnp.concatenate([jnp.zeros_like(head), head], axis=0),
            jnp.concatenate([head, rest], axis=0),
        ], axis=1)
        return jnp.dot(left, right, preferred_element_type=F32)

    def main_store(c, product):
        at = lanes_of(c)
        z[first, at] = pick_groups(product[:, :LANES], groups, taps)
        late = q1[second, at].astype(F32) * pick_groups(product[:, LANES:], groups, taps)
        z[second, at] = late
        squares[core, second, :] += late * late

    make_tables(0, 0)

    @pl.loop(0, chunks // 2)
    def _(pair):
        c = 2 * pair
        product = main_product(c, 0)
        make_tables(c + 1, 1)
        main_store(c, product)
        product = main_product(c + 1, 1)
        make_tables(lax.rem(c + 2, chunks), 0)
        main_store(c + 1, product)

    segment = lax.broadcasted_iota(jnp.int32, (SEGS, LANES), 0)
    halves = (first, second)

    def square_copy(h, k, slot):
        rows = pl.ds(h * taps, taps)
        return pltpu.make_async_remote_copy(
            src_ref=squares.at[core, rows], dst_ref=squares.at[slot, rows],
            send_sem=sq_send.at[h, k], recv_sem=sq_recv.at[h, slot],
            device_id={"tp": lax.rem(core + k, tp_size)}, device_id_type=MESH,
        )

    def send_squares(h):
        @pl.loop(1, tp_size)
        def _(k):
            square_copy(h, k, core).start()

    def find_scale(h):
        @pl.loop(1, tp_size)
        def _(k):
            square_copy(h, k, lax.rem(core + k, tp_size)).wait_recv()
        total = squares[0, halves[h], :]
        for i in range(1, tp_size):
            total = total + squares[i, halves[h], :]
        total = jnp.sum(total, axis=1, keepdims=True)
        scale[halves[h], :] = jnp.broadcast_to(lax.rsqrt(total / D + 1e-06), (taps, LANES))

    def decays(at):
        return [jnp.broadcast_to(decay_one[m : m + 1, at], (SEGS, LANES)) for m in range(modes)]

    def set_signal(h, at, i):
        scaled = z[halves[h], at] * scale[halves[h], :] * gain_ref[:, at]
        u_two = (k2[halves[h], at].astype(F32) * scaled).astype(BF16).astype(F32)
        z[halves[h], at] = u_two
        u_wide[i] = u_two

    zero_states = (jnp.zeros((SEGS, LANES), F32),) * modes

    def local_pass(h, at, i):
        decay = decays(at)
        weight = [jnp.broadcast_to(weights[m : m + 1, at], (SEGS, LANES)) for m in range(modes)]

        def step(t, states):
            rows = pl.ds(t, SEGS, stride=steps)
            x = u_wide[i, rows, :]
            states = tuple(decay[m] * states[m] + x for m in range(modes))
            terms = [weight[m] * states[m] for m in range(modes)]
            while len(terms) > 1:
                terms = [a + b for a, b in zip(terms[::2], terms[1::2])]
            y_wide[i, rows, :] = terms[0]
            return states

        states = lax.fori_loop(0, steps, step, zero_states, unroll=8)
        y[halves[h], at] = y_wide[i, :taps, :]
        return states

    def closing_pass(at, i):
        decay = decays(at)

        def step(t, states):
            x = u_wide[i, pl.ds(t, SEGS, stride=steps), :]
            return tuple(decay[m] * states[m] + x for m in range(modes))

        return lax.fori_loop(0, steps, step, zero_states, unroll=16)

    def join_segments(h, at, m, inclusive):
        factor = jnp.broadcast_to(decay_seg[m : m + 1, at], (SEGS, LANES))
        shift = 1
        while shift < SEGS:
            moved = jnp.where(segment >= shift, pltpu.roll(inclusive, shift, 0), 0.0)
            inclusive = inclusive + factor * moved
            factor = factor * factor
            shift *= 2
        prior[h, m * SEGS : (m + 1) * SEGS, at] = jnp.where(
            segment >= 1, pltpu.roll(inclusive, 1, 0), 0.0
        )
        return inclusive[SEGS - 1 :, :]

    send_squares(1)

    @pl.loop(0, chunks)
    def _(c):
        at = lanes_of(c)
        double = 2.0 * rate_ref[:, at]
        series = jnp.ones_like(double)
        for order in range(10, 1, -1):
            series = 1.0 - double * series * (1.0 / order)
        gap = jnp.where(double < 0.5, double * series, 1.0 - jnp.exp(-double))
        weights[:, at] = residue_ref[:, at] * jnp.sqrt(gap)
        decay_one[:, at] = jnp.exp(-rate_ref[:, at])
        per_segment = jnp.exp(-rate_ref[:, at] * steps)
        decay_seg[:, at] = per_segment
        per_half = per_segment
        for _ in range(3):
            per_half = per_half * per_half
        decay_half[:, at] = per_half

    loads[5].wait()
    find_scale(1)

    @pl.loop(0, chunks // 2)
    def _(pair):
        for i in range(2):
            at = lanes_of(2 * pair + i)
            set_signal(1, at, i)
            states = local_pass(1, at, i)
            for m in range(modes):
                last = join_segments(1, at, m, states[m])
                late_state[m : m + 1, at] = last

    pairs = chunks // PIECES // 2
    for p in range(PIECES):
        @pl.when(me > 0)
        def _():
            halo_copy(p).wait_recv()

        @pl.loop(p * pairs, (p + 1) * pairs)
        def _(pair):
            left = jnp.concatenate([early[2 * pair], early[2 * pair + 1]], axis=1)
            one, two = halo[:, lanes_of(2 * pair)], halo[:, lanes_of(2 * pair + 1)]
            zero = jnp.zeros_like(one)
            right = jnp.concatenate([
                jnp.concatenate([one, zero], axis=0), jnp.concatenate([zero, two], axis=0)
            ], axis=1)
            product = jnp.dot(left, right, preferred_element_type=F32)
            for i in range(2):
                at = lanes_of(2 * pair + i)
                conv = z[first, at] + pick_groups(product[:, i * LANES : (i + 1) * LANES], groups, taps)
                value = q1[first, at].astype(F32) * conv
                z[first, at] = value
                squares[core, first, :] += value * value

    send_squares(0)
    find_scale(0)

    def in_copy(j):
        return pltpu.make_async_remote_copy(
            src_ref=state.at[j], dst_ref=inbox.at[me],
            send_sem=in_send.at[j], recv_sem=in_recv.at[me],
            device_id={"ctx": j}, device_id_type=MESH,
        )

    @pl.loop(0, owners)
    def _(k):
        j = lax.rem(me + 1 + k, owners)
        for i in range(per_owner):
            at = lanes_of(j * per_owner + i)
            set_signal(0, at, i)
            states = closing_pass(at, i)
            for m in range(modes):
                last = join_segments(0, at, m, states[m])
                early_state[m : m + 1, at] = last
            closing = decay_half[:, at] * early_state[:, at] + late_state[:, at]
            state[j, :, i * LANES : (i + 1) * LANES] = closing.astype(BF16)

        @pl.when(j != me)
        def _():
            in_copy(j).start()

    def local_first(start, stop):
        @pl.loop(start, stop)
        def _(pair):
            for i in range(2):
                at = lanes_of(2 * pair + i)
                u_wide[i] = z[first, at]
                local_pass(0, at, i)

    def in_arrival(d):
        return pltpu.make_async_remote_copy(
            src_ref=state.at[0], dst_ref=inbox.at[d],
            send_sem=in_send.at[0], recv_sem=in_recv.at[d],
            device_id={"ctx": d}, device_id_type=MESH,
        )

    def back_copy(d):
        return pltpu.make_async_remote_copy(
            src_ref=outbox.at[d], dst_ref=incoming.at[me],
            send_sem=back_send.at[d], recv_sem=back_recv.at[me],
            device_id={"ctx": d}, device_id_type=MESH,
        )

    def back_arrival(j):
        return pltpu.make_async_remote_copy(
            src_ref=outbox.at[0], dst_ref=incoming.at[j],
            send_sem=back_send.at[0], recv_sem=back_recv.at[j],
            device_id={"ctx": j}, device_id_type=MESH,
        )

    early_pairs = chunks // 4
    local_first(0, early_pairs)

    @pl.when(me < owners)
    def _():
        inbox[me] = state[lax.rem(me, owners)]
        mine = pl.ds(pl.multiple_of(lax.rem(me, owners) * own, own), own)
        stride = jnp.exp(-rate_ref[:, mine] * length)

        def pass_on(d, running):
            @pl.when(d != me)
            def _():
                in_arrival(d).wait_recv()
            sent = running.astype(BF16)
            outbox[d] = sent

            @pl.when(d != me)
            def _():
                back_copy(d).start()

            @pl.when(d == me)
            def _():
                incoming[lax.rem(me, owners)] = sent
            return stride * running + inbox[d].astype(F32)

        lax.fori_loop(0, ctx_size, pass_on, jnp.zeros((modes, own), F32))

    local_first(early_pairs, chunks // 2)
    loads[6].wait()

    def out_copy(j):
        cols = pl.ds(pl.multiple_of(j * own, own), own)
        return pltpu.make_async_copy(out.at[:, cols], out_hbm.at[:, cols], out_sem.at[j])

    @pl.loop(0, owners)
    def _(j):
        @pl.when(j != me)
        def _():
            back_arrival(j).wait_recv()
        for i in range(per_owner):
            at = lanes_of(j * per_owner + i)
            decay = decays(at)
            arrived = incoming[j, :, i * LANES : (i + 1) * LANES].astype(F32)
            later = early_state[:, at] + decay_half[:, at] * arrived
            weight = weights[:, at]
            heads = ([], [])
            for m in range(modes):
                one = jnp.broadcast_to(decay_seg[m : m + 1, at], (SEGS, LANES))
                two = one * one
                lift = jnp.where(segment % 2 == 1, one, 1.0)
                lift = lift * jnp.where(segment // 2 % 2 == 1, two, 1.0)
                lift = lift * jnp.where(segment // 4 % 2 == 1, two * two, 1.0)
                for h, carried in enumerate((arrived, later)):
                    begin = prior[h, m * SEGS : (m + 1) * SEGS, at] + lift * carried[m : m + 1, :]
                    heads[h].append(weight[m : m + 1, :] * begin)
            entering = heads[0] + heads[1]

            def step(t, entering):
                entering = tuple(decay[m % modes] * entering[m] for m in range(2 * modes))
                for h in range(2):
                    terms = entering[h * modes : (h + 1) * modes]
                    while len(terms) > 1:
                        terms = [a + b for a, b in zip(terms[::2], terms[1::2])]
                    y_wide[i, pl.ds(h * taps + t, SEGS, stride=steps), :] = terms[0]
                return entering

            lax.fori_loop(0, steps, step, tuple(entering), unroll=8)
            out[:, at] = (q2[:, at].astype(F32) * (y[:, at] + y_wide[i])).astype(BF16)
        out_copy(j).start()

    @pl.loop(0, owners)
    def _(j):
        out_copy(j).wait()

        @pl.when(j != me)
        def _():
            in_copy(j).wait_send()

    @pl.when(me < owners)
    def _():
        @pl.loop(0, ctx_size)
        def _(d):
            @pl.when(d != me)
            def _():
                back_copy(d).wait_send()

    @pl.loop(1, tp_size)
    def _(k):
        square_copy(0, k, core).wait_send()
        square_copy(1, k, core).wait_send()

    @pl.when(me < ctx_size - 1)
    def _():
        for p in range(PIECES):
            halo_copy(p).wait_send()


def on_device(q_one, k_one, v_one, mr_filter, norm_gain, q_two, k_two, li_rates, li_residues):
    length, channels = q_one.shape
    filters, taps = mr_filter.shape
    modes = li_rates.shape[0]
    ctx_size, tp_size = lax.axis_size("ctx"), lax.axis_size("tp")
    owners = min(ctx_size, channels // LANES)
    own = channels // owners
    chunks = channels // LANES
    table_rows = filters // chunks * taps
    wide = pltpu.VMEM((length, channels), BF16)
    dma = pltpu.SemaphoreType.DMA
    anywhere = pl.BlockSpec(memory_space=pl.ANY)
    inside = pl.BlockSpec(memory_space=pltpu.VMEM)
    return pl.pallas_call(
        functools.partial(whole_kernel, ctx_size, tp_size, owners),
        in_specs=[anywhere] * 5 + [inside] * 4,
        out_specs=anywhere,
        out_shape=jax.ShapeDtypeStruct((length, channels), BF16),
        scratch_shapes=[
            wide, wide, wide, wide, wide, wide, wide,
            pltpu.VMEM((taps, channels), BF16),
            pltpu.VMEM((length, channels), F32),
            pltpu.VMEM((chunks, table_rows, taps), BF16),
            pltpu.VMEM((2, table_rows, taps), BF16),
            pltpu.VMEM((filters, taps), F32),
            pltpu.VMEM((tp_size, length, LANES), F32),
            pltpu.VMEM((length, LANES), F32),
            pltpu.VMEM((max(2, own // LANES), taps, LANES), F32),
            pltpu.VMEM((max(2, own // LANES), length, LANES), F32),
            pltpu.VMEM((length, channels), F32),
            pltpu.VMEM((modes, channels), F32),
            pltpu.VMEM((2, modes * SEGS, channels), F32),
            pltpu.VMEM((modes, channels), F32),
            pltpu.VMEM((modes, channels), F32),
            pltpu.VMEM((modes, channels), F32),
            pltpu.VMEM((modes, channels), F32),
            pltpu.VMEM((modes, channels), F32),
            pltpu.VMEM((owners, modes, own), BF16),
            pltpu.VMEM((ctx_size, modes, own), BF16),
            pltpu.VMEM((ctx_size, modes, own), BF16),
            pltpu.VMEM((owners, modes, own), BF16),
            dma((7,)), dma((PIECES,)), dma((PIECES,)), dma((2, tp_size)), dma((2, tp_size)),
            dma((owners,)), dma((ctx_size,)), dma((ctx_size,)), dma((owners,)), dma((owners,)),
        ],
        compiler_params=pltpu.CompilerParams(
            vmem_limit_bytes=60 << 20, collective_id=0, has_side_effects=True
        ),
    )(q_one, k_one, v_one, q_two, k_two, mr_filter, norm_gain[None, :], li_rates, li_residues)


def solution(mesh):
    in_specs = (
        P("ctx", "tp"),
        P("ctx", "tp"),
        P("ctx", "tp"),
        P("tp", None),
        P("tp"),
        P("ctx", "tp"),
        P("ctx", "tp"),
        P(None, "tp"),
        P(None, "tp"),
    )
    out_specs = P("ctx", "tp")
    return jax.shard_map(
        on_device, mesh=mesh, in_specs=in_specs, out_specs=out_specs, check_vma=False
    )
```
